32 devices in a mesh: dp: 16 (over z, x, core), tensor: 2 (over y).
Axes of the slice: x: 2, y: 2, z: 4, core: 2. Of those that a mesh axis runs over, the one named last changes fastest.
Arguments:
- inputs: bfloat16 [16384, 1024], P(('dp', 'tensor')), may hold values from -6 to 6
- qkv_weight: bfloat16 [1024, 3072], P('dp', 'tensor'), may hold values from -0.1875 to 0.1875
- qv_bias: float32 [2048], P('tensor'), may hold values from -3 to 3
- out_weight: bfloat16 [1024, 1024], P('tensor', 'dp'), may hold values from -1 to 1
- out_bias: float32 [1024], replicated, may hold values from -2 to 2
- up_weight: bfloat16 [1024, 4096], P('dp', 'tensor'), may hold values from -0.1875 to 0.1875
- up_bias: float32 [4096], P('tensor'), may hold values from -3 to 3
- down_weight: bfloat16 [4096, 1024], P('tensor', 'dp'), may hold values from -0.125 to 0.125
- down_bias: float32 [1024], replicated, may hold values from -2 to 2
- gain_one: float32 [1024], replicated, may hold values from 0.25 to 1.75
- shift_one: float32 [1024], replicated, may hold values from -2 to 2
- gain_two: float32 [1024], replicated, may hold values from 0.25 to 1.75
- shift_two: float32 [1024], replicated, may hold values from -2 to 2
- cotangent: bfloat16 [16384, 1024], P(('dp', 'tensor')), may hold values from -6 to 6
Outputs:
- layer_out: bfloat16 [16384, 1024], P(('dp', 'tensor'))
- input_grad: float32 [16384, 1024], P(('dp', 'tensor'))
- qkv_weight_grad: float32 [1024, 3072], P('dp', 'tensor')
- qv_bias_grad: float32 [2048], P('tensor')
- out_weight_grad: float32 [1024, 1024], P('tensor', 'dp')
- out_bias_grad: float32 [1024], replicated
- up_weight_grad: float32 [1024, 4096], P('dp', 'tensor')
- up_bias_grad: float32 [4096], P('tensor')
- down_weight_grad: float32 [4096, 1024], P('tensor', 'dp')
- down_bias_grad: float32 [1024], replicated
- gain_one_grad: float32 [1024], replicated
- shift_one_grad: float32 [1024], replicated
- gain_two_grad: float32 [1024], replicated
- shift_two_grad: float32 [1024], replicated
The draws below stay inside these ranges and needn't reach their ends.
All inputs are finite; a program needn't handle non-finite values.
Results may differ from the reference program's by a relative error of at most 0.015.
Values may be sent and summed in bfloat16 or wider, within the bound.
A program may use at most 192 MiB of HBM per device.

```python
import math
import jax
import jax.numpy as jnp
from jax import lax

D = 1024
HEADS = 16
HD = 64
FF = 4096
LEN = 1024
TOKENS = 16384


def raised(values, stream_key, source, target, parts, factor):
    owner, partner = [(jnp.arange(values.shape[axis_at]) // (values.shape[axis_at] // parts)).reshape([-1 if axis == axis_at else 1 for axis in range(values.ndim)]) for axis_at in (source, target)]
    chosen = jax.random.permutation(stream_key, parts)[partner]
    strong = (owner == chosen) | (owner == (partner + parts // 2) % parts)
    return jnp.where(strong, factor * values, values)


def block_scale(key, shape, shards, smallest, top_value):
    factor_of = 1.0
    for position, blocks in shards:
        draws = jax.random.uniform(jax.random.fold_in(jax.random.fold_in(key, 6), position), (blocks,), jnp.float32, smallest / len(shards), top_value / len(shards))
        factor_of = factor_of * jnp.repeat(jnp.exp(draws), shape[position] // blocks).reshape((-1,) + (1,) * (len(shape) - 1 - position))
    return factor_of


def noise(stream_key, extent, deviation, limit, shards=(), kind=jnp.bfloat16):
    factor_of = block_scale(stream_key, extent, shards, -0.22, 0.18) if shards else 1.0
    drawn = jax.random.normal(stream_key, extent, jnp.float32) * deviation * factor_of
    return jnp.minimum(jnp.maximum(drawn, -limit), limit).astype(kind)


def heavy_noise(rng, shape, deviation, bound, pieces, heavy, kind=jnp.bfloat16):
    entries = deviation * jax.random.normal(rng, shape, jnp.float32)
    if pieces:
        entries = entries * block_scale(rng, shape, pieces, -0.22, 0.18)
    return jnp.clip(raised(entries, jax.random.fold_in(rng, 3), *heavy), -bound, bound).astype(kind)


def setup_inputs(seed: int = 0) -> dict:
    streams_of = jax.random.split(jax.random.key(seed), 15)
    inputs = heavy_noise(streams_of[0], (TOKENS, D), 1.0, 6.0, ((0, 32),), (0, 1, 32, 2.75))
    qkv_weight = noise(streams_of[1], (D, 3 * D), D ** -0.5, 0.1875, ((0, 16), (1, 2)))
    qv_bias = noise(streams_of[2], (2 * D,), 0.5, 3.0, ((0, 2),), jnp.float32)
    out_weight = noise(streams_of[3], (D, D), (max(D // 32, 1)) ** -0.5, 1.0, ((0, 2), (1, 16)))
    out_bias = noise(streams_of[4], (D,), 0.3, 2.0, (), jnp.float32)
    up_weight = noise(streams_of[5], (D, FF), D ** -0.5, 0.1875, ((0, 16), (1, 2)))
    up_bias = noise(streams_of[6], (FF,), 0.5, 3.0, ((0, 2),), jnp.float32)
    down_weight = noise(streams_of[7], (FF, D), (FF // 2) ** -0.5, 0.125, ((0, 2), (1, 16)))
    down_bias = noise(streams_of[8], (D,), 0.3, 2.0, (), jnp.float32)
    gain_one = jnp.clip(1.0 + 0.15 * jax.random.normal(streams_of[9], (D,), jnp.float32), 0.25, 1.75)
    shift_one = noise(streams_of[10], (D,), 0.3, 2.0, (), jnp.float32)
    gain_two = jnp.clip(1.0 + 0.15 * jax.random.normal(streams_of[11], (D,), jnp.float32), 0.25, 1.75)
    shift_two = noise(streams_of[12], (D,), 0.3, 2.0, (), jnp.float32)
    cotangent = heavy_noise(streams_of[13], (TOKENS, D), 1.0, 6.0, ((0, 32),), (0, 1, 32, 2.75))
    return {"inputs": inputs, "qkv_weight": qkv_weight, "qv_bias": qv_bias, "out_weight": out_weight, "out_bias": out_bias, "up_weight": up_weight, "up_bias": up_bias, "down_weight": down_weight, "down_bias": down_bias, "gain_one": gain_one, "shift_one": shift_one, "gain_two": gain_two, "shift_two": shift_two, "cotangent": cotangent}


@jax.custom_vjp
def low(v):
    return lax.optimization_barrier(v.astype(jnp.bfloat16)).astype(jnp.float32)

@jax.custom_vjp
def low_back(v):
    return v

def low_keep(v):
    return (low(v), None)

def low_pass(kept, grad):
    return (grad,)

def back_keep(v):
    return (v, None)

def back_low(kept, grad):
    return (low(grad),)
low.defvjp(low_keep, low_pass)
low_back.defvjp(back_keep, back_low)
eps = 1e-05
highest = lax.Precision.HIGHEST

def normalize(values_in, gain_vec, shift_vec):
    row_mean = lax.optimization_barrier(jnp.mean(values_in, axis=-1, keepdims=True))
    centred = values_in - row_mean
    row_var = lax.optimization_barrier(jnp.mean(centred * centred, axis=-1, keepdims=True))
    return centred * lax.rsqrt(row_var + eps) * gain_vec + shift_vec

def rounded(values_in):
    return low(low_back(values_in))

def attend(queries, key_rows, value_rows):
    length = queries.shape[0]
    block_rows = min(512, length)
    block_count = length // block_rows
    score_scale = 1.0 / math.sqrt(queries.shape[-1])
    query_blocks = queries.reshape(block_count, block_rows, queries.shape[1], queries.shape[2])

    def block_attend(pair_in):
        query_block, block_idx = pair_in
        raw_scores = jnp.einsum('qhe,khe->hqk', query_block, key_rows, precision=highest)
        scores = low_back(raw_scores * score_scale)
        row_ids = block_idx * block_rows + jnp.arange(block_rows)
        allowed = jnp.arange(length)[None, :] <= row_ids[:, None]
        scores = jnp.where(allowed[None], scores, -1e+30)
        row_peak = lax.optimization_barrier(jnp.max(scores, axis=-1, keepdims=True))
        exp_scores = jnp.exp(scores - row_peak)
        probs_low = low(exp_scores / lax.optimization_barrier(jnp.sum(exp_scores, axis=-1, keepdims=True)))
        return jnp.einsum('hqk,khe->qhe', probs_low, value_rows, precision=highest)
    outputs = lax.map(jax.checkpoint(block_attend), (query_blocks, jnp.arange(block_count)))
    return outputs.reshape(length, queries.shape[1], queries.shape[2])

def layer(rows_in, qkv_weight, qv_bias, out_weight, out_bias, up_weight, up_bias, down_weight, down_bias, gain_one, shift_one, gain_two, shift_two):
    length = rows_in.shape[0]
    normed = low(normalize(rows_in, gain_one, shift_one))
    mixed_qkv = jnp.dot(normed, qkv_weight, precision=highest).reshape(length, HEADS, 3, HD)
    biases = qv_bias.reshape(HEADS, 2, HD)
    queries = rounded(mixed_qkv[:, :, 0] + biases[:, 0])
    key_rows = rounded(mixed_qkv[:, :, 1])
    value_rows = rounded(mixed_qkv[:, :, 2] + biases[:, 1])
    heads_out = rounded(attend(queries, key_rows, value_rows)).reshape(length, D)
    branch = low_back(jnp.dot(heads_out, out_weight, precision=highest) + out_bias)
    middle = rows_in + branch
    second = low(normalize(middle, gain_two, shift_two))
    hidden = low_back(jnp.dot(second, up_weight, precision=highest) + up_bias)
    active = low(jax.nn.gelu(hidden, approximate=True))
    down_out = low_back(jnp.dot(active, down_weight, precision=highest) + down_bias)
    return middle + down_out

def reference(inputs, qkv_weight, qv_bias, out_weight, out_bias, up_weight, up_bias, down_weight, down_bias, gain_one, shift_one, gain_two, shift_two, cotangent):
    params = tuple((param.astype(jnp.float32) for param in (qkv_weight, qv_bias, out_weight, out_bias, up_weight, up_bias, down_weight, down_bias, gain_one, shift_one, gain_two, shift_two)))
    seq_count = inputs.shape[0] // LEN
    seq_inputs = inputs.astype(jnp.float32).reshape(seq_count, LEN, D)
    seq_cots = cotangent.astype(jnp.float32).reshape(seq_count, LEN, D)

    def per_sequence(totals, pair_in):
        rows_in, cot_rows = pair_in
        result, pullback = jax.vjp(layer, rows_in, *params)
        grads = pullback(cot_rows)
        totals = tuple((accum + fresh for accum, fresh in zip(totals, grads[1:])))
        return (totals, (result, grads[0]))
    zero_init = tuple((jnp.zeros_like(param) for param in params))
    totals, (results, row_grads) = lax.scan(per_sequence, zero_init, (seq_inputs, seq_cots))
    layer_out = results.reshape(-1, D).astype(jnp.bfloat16)
    input_grad = row_grads.reshape(-1, D)
    return (layer_out, input_grad, totals[0], totals[1], totals[2], totals[3], totals[4], totals[5], totals[6], totals[7], totals[8], totals[9], totals[10], totals[11])
```

```python
import jax
import jax.numpy as jnp
from jax import lax
from jax.experimental import pallas as pl
from jax.experimental.pallas import tpu as pltpu
from jax.sharding import PartitionSpec as P

HD = 64
LEN = 1024
QB = 256
SCALE = 0.125
NEG = -1e30
F32 = jnp.float32
BF16 = jnp.bfloat16


eps = 1e-05


def normalize(values_in, gain_vec, shift_vec):
    row_mean = jnp.mean(values_in, axis=-1, keepdims=True)
    centred = values_in - row_mean
    row_var = jnp.mean(centred * centred, axis=-1, keepdims=True)
    return centred * lax.rsqrt(row_var + eps) * gain_vec + shift_vec


def gelu_tanh(hidden):
    return jax.nn.gelu(hidden, approximate=True)


def dot(left, right):
    return jnp.dot(left, right, preferred_element_type=F32)


def contract_rows(left, right):
    return lax.dot_general(left, right, (((0,), (0,)), ((), ())), preferred_element_type=F32)


def contract_cols(left, right):
    return lax.dot_general(left, right, (((1,), (1,)), ((), ())), preferred_element_type=F32)


def probs_columns(query_block, keys, first_row):
    scores = contract_cols(keys, query_block)
    key_ids = lax.broadcasted_iota(jnp.int32, scores.shape, 0)
    row_ids = first_row + lax.broadcasted_iota(jnp.int32, scores.shape, 1)
    scores = jnp.where(key_ids <= row_ids, scores, NEG)
    exp_scores = jnp.exp(scores - jnp.max(scores, axis=0, keepdims=True))
    return exp_scores * (1.0 / jnp.sum(exp_scores, axis=0, keepdims=True))


def forward_kernel(qkv_ref, out_ref):
    for head in range(2):
        base = head * 3 * HD
        for block in range(LEN // QB):
            lo, hi = block * QB, (block + 1) * QB
            queries = qkv_ref[lo:hi, base : base + HD] * SCALE
            keys = qkv_ref[:hi, base + HD : base + 2 * HD]
            values = qkv_ref[:hi, base + 2 * HD : base + 3 * HD]
            probs = probs_columns(queries, keys, lo).astype(BF16)
            out_ref[lo:hi, head * HD : (head + 1) * HD] = contract_rows(values, probs).T.astype(BF16)


def backward_kernel(qkv_ref, grad_ref, out_ref, key_acc, value_acc):
    for head in range(2):
        base = head * 3 * HD
        for block in reversed(range(LEN // QB)):
            lo, hi = block * QB, (block + 1) * QB
            queries = qkv_ref[lo:hi, base : base + HD] * SCALE
            keys = qkv_ref[:hi, base + HD : base + 2 * HD]
            values = qkv_ref[:hi, base + 2 * HD : base + 3 * HD]
            grads = grad_ref[lo:hi, head * HD : (head + 1) * HD]
            probs = probs_columns(queries, keys, lo)
            prob_grad = contract_cols(values, grads)
            row_dot = jnp.sum(probs * prob_grad, axis=0, keepdims=True)
            score_grad = (probs * (prob_grad - row_dot)).astype(BF16)
            query_grad = (contract_rows(keys, score_grad) * SCALE).T
            out_ref[lo:hi, base : base + HD] = query_grad.astype(BF16)
            key_part = dot(score_grad, queries)
            value_part = dot(probs.astype(BF16), grads)
            if hi == LEN:
                key_acc[...] = key_part
                value_acc[...] = value_part
            else:
                key_acc[:hi, :] += key_part
                value_acc[:hi, :] += value_part
        out_ref[:, base + HD : base + 2 * HD] = key_acc[...].astype(BF16)
        out_ref[:, base + 2 * HD : base + 3 * HD] = value_acc[...].astype(BF16)


def attention_cost(qkv, products):
    rows, columns = qkv.shape
    pairs = rows * LEN * (columns // (3 * HD))
    return pl.CostEstimate(
        flops=products * pairs * HD * 4, bytes_accessed=4 * rows * columns, transcendentals=pairs
    )


def attend_forward(qkv):
    rows, columns = qkv.shape
    return pl.pallas_call(
        forward_kernel,
        grid=(rows // LEN, columns // (6 * HD)),
        in_specs=[pl.BlockSpec((LEN, 6 * HD), lambda s, h: (s, h))],
        out_specs=pl.BlockSpec((LEN, 2 * HD), lambda s, h: (s, h)),
        out_shape=jax.ShapeDtypeStruct((rows, columns // 3), BF16),
        compiler_params=pltpu.CompilerParams(vmem_limit_bytes=40 * 2**20),
        cost_estimate=attention_cost(qkv, 2),
    )(qkv)


def attend_backward(qkv, heads_grad):
    rows, columns = qkv.shape
    return pl.pallas_call(
        backward_kernel,
        grid=(rows // LEN, columns // (6 * HD)),
        in_specs=[
            pl.BlockSpec((LEN, 6 * HD), lambda s, h: (s, h)),
            pl.BlockSpec((LEN, 2 * HD), lambda s, h: (s, h)),
        ],
        out_specs=pl.BlockSpec((LEN, 6 * HD), lambda s, h: (s, h)),
        out_shape=jax.ShapeDtypeStruct((rows, columns), BF16),
        scratch_shapes=[pltpu.VMEM((LEN, HD), F32), pltpu.VMEM((LEN, HD), F32)],
        compiler_params=pltpu.CompilerParams(vmem_limit_bytes=40 * 2**20),
        cost_estimate=attention_cost(qkv, 5),
    )(qkv, heads_grad)


def swap(values):
    return lax.ppermute(values, "tensor", [(0, 1), (1, 0)])


def total_over(values, axis):
    size = lax.axis_size(axis)
    if size & (size - 1):
        return lax.psum(values, axis)
    step = 1
    while step < size:
        values = values + lax.ppermute(values, axis, [(i, i ^ step) for i in range(size)])
        step *= 2
    return values


class Pair:
    def __init__(self):
        self.first = lax.axis_index("tensor") == 0

    def gather(self, mine):
        return (mine, swap(mine))

    def ordered(self, parts):
        mine, other = parts
        return jnp.where(
            self.first, jnp.concatenate((mine, other)), jnp.concatenate((other, mine))
        )

    def split(self, rows):
        top, low = jnp.split(rows, 2)
        return (jnp.where(self.first, top, low), jnp.where(self.first, low, top))

    def scatter(self, parts, product):
        mine, other = parts
        theirs = swap(product(other).astype(BF16))
        return product(mine) + theirs.astype(F32)


class Group:
    def gather(self, mine):
        return (lax.all_gather(mine, "tensor", axis=0, tiled=True),)

    def ordered(self, parts):
        return parts[0]

    def split(self, rows):
        return (rows,)

    def scatter(self, parts, product):
        summed = lax.psum_scatter(
            product(parts[0]).astype(BF16), "tensor", scatter_dimension=0, tiled=True
        )
        return summed.astype(F32)


def shards(
    inputs,
    qkv_weight,
    qv_bias,
    out_weight,
    out_bias,
    up_weight,
    up_bias,
    down_weight,
    down_bias,
    gain_one,
    shift_one,
    gain_two,
    shift_two,
    cotangent,
):
    group = Pair() if lax.axis_size("tensor") == 2 else Group()
    join = lambda parts: jnp.concatenate(parts) if len(parts) > 1 else parts[0]
    each = lambda fn, parts: tuple(fn(part) for part in parts)
    local_x = inputs.astype(F32)
    head_count = qv_bias.shape[0] // (2 * HD)
    first_norm = normalize(local_x, gain_one, shift_one).astype(BF16)
    first_parts = group.gather(first_norm)
    qkv_full = lax.all_gather(qkv_weight, "dp", axis=0, tiled=True)
    out_full = lax.all_gather(out_weight, "dp", axis=1, tiled=True)
    up_full = lax.all_gather(up_weight, "dp", axis=0, tiled=True)
    down_full = lax.all_gather(down_weight, "dp", axis=1, tiled=True)
    biases = qv_bias.reshape(head_count, 2, HD)
    qkv_bias = jnp.stack(
        (biases[:, 0], jnp.zeros_like(biases[:, 0]), biases[:, 1]), axis=1
    ).reshape(-1)
    qkv = group.ordered(
        each(lambda rows: (dot(rows, qkv_full) + qkv_bias).astype(BF16), first_parts)
    )
    heads_low = attend_forward(qkv)
    heads_parts = group.split(heads_low)
    branch = group.scatter(heads_parts, lambda rows: dot(rows, out_full)) + out_bias
    middle = local_x + branch
    second_norm = normalize(middle, gain_two, shift_two).astype(BF16)
    second_parts = group.gather(second_norm)
    hidden = each(lambda rows: dot(rows, up_full) + up_bias, second_parts)
    active = each(lambda rows: gelu_tanh(rows).astype(BF16), hidden)
    down_out = group.scatter(active, lambda rows: dot(rows, down_full)) + down_bias
    layer_out = (middle + down_out).astype(BF16)

    out_grad = cotangent.astype(F32)
    down_bias_grad = jnp.sum(out_grad, axis=0)
    down_parts = group.gather(cotangent)

    def hidden_back(pair_in):
        rows, grads = pair_in
        active_grad = contract_cols(grads, down_full)
        return jax.vjp(gelu_tanh, rows)[1](active_grad)[0].astype(BF16)

    hidden_parts = each(hidden_back, tuple(zip(hidden, down_parts)))
    second_grad = group.scatter(hidden_parts, lambda rows: contract_cols(rows, up_full))
    down_weight_grad = contract_rows(join(active), join(down_parts)).astype(BF16)
    down_shard = lax.psum_scatter(down_weight_grad, "dp", scatter_dimension=1, tiled=True)
    hidden_low = join(hidden_parts)
    up_bias_grad = jnp.sum(hidden_low, axis=0, dtype=F32)
    up_weight_grad = contract_rows(join(second_parts), hidden_low).astype(BF16)
    up_shard = lax.psum_scatter(up_weight_grad, "dp", scatter_dimension=0, tiled=True)
    norm_pull = jax.vjp(normalize, middle, gain_two, shift_two)[1]
    middle_part, gain_two_grad, shift_two_grad = norm_pull(second_grad)
    middle_grad = out_grad + middle_part
    branch_low = middle_grad.astype(BF16)
    out_bias_grad = jnp.sum(branch_low, axis=0, dtype=F32)
    branch_parts = group.gather(branch_low)
    heads_grad = group.ordered(
        each(lambda rows: contract_cols(rows, out_full).astype(BF16), branch_parts)
    )
    out_weight_grad = contract_rows(join(heads_parts), join(branch_parts)).astype(BF16)
    out_shard = lax.psum_scatter(out_weight_grad, "dp", scatter_dimension=1, tiled=True)
    qkv_low = attend_backward(qkv, heads_grad)
    qkv_parts = group.split(qkv_low)
    qkv_weight_grad = contract_rows(join(first_parts), join(qkv_parts)).astype(BF16)
    qkv_shard = lax.psum_scatter(qkv_weight_grad, "dp", scatter_dimension=0, tiled=True)
    first_grad = group.scatter(qkv_parts, lambda rows: contract_cols(rows, qkv_full))
    bias_sums = jnp.sum(qkv_low, axis=0, dtype=F32).reshape(head_count, 3, HD)
    qv_bias_grad = jnp.stack((bias_sums[:, 0], bias_sums[:, 2]), axis=1).reshape(-1)
    first_pull = jax.vjp(normalize, local_x, gain_one, shift_one)[1]
    input_part, gain_one_grad, shift_one_grad = first_pull(first_grad)
    input_grad = middle_grad + input_part

    width = out_bias.shape[0]
    shared = jnp.concatenate(
        (
            out_bias_grad,
            down_bias_grad,
            gain_two_grad,
            shift_two_grad,
            gain_one_grad,
            shift_one_grad,
        )
    )
    owned = jnp.concatenate((qv_bias_grad, up_bias_grad))
    shared = total_over(shared, "tensor")
    totals = total_over(jnp.concatenate((shared, owned)).reshape(-1, 128), "dp").reshape(-1)
    out_bias_total, down_bias_total, gain_two_total, shift_two_total, gain_one_total, shift_one_total = (
        jnp.split(totals[: 6 * width], 6)
    )
    qv_bias_total, up_bias_total = jnp.split(totals[6 * width :], [qv_bias.shape[0]])
    return (
        layer_out,
        input_grad,
        qkv_shard.astype(F32),
        qv_bias_total,
        out_shard.astype(F32),
        out_bias_total,
        up_shard.astype(F32),
        up_bias_total,
        down_shard.astype(F32),
        down_bias_total,
        gain_one_total,
        shift_one_total,
        gain_two_total,
        shift_two_total,
    )


def solution(mesh):
    in_specs = (
        P(("dp", "tensor"), None),
        P("dp", "tensor"),
        P("tensor"),
        P("tensor", "dp"),
        P(),
        P("dp", "tensor"),
        P("tensor"),
        P("tensor", "dp"),
        P(),
        P(),
        P(),
        P(),
        P(),
        P(("dp", "tensor"), None),
    )
    out_specs = (
        P(("dp", "tensor"), None),
        P(("dp", "tensor"), None),
        P("dp", "tensor"),
        P("tensor"),
        P("tensor", "dp"),
        P(),
        P("dp", "tensor"),
        P("tensor"),
        P("tensor", "dp"),
        P(),
        P(),
        P(),
        P(),
        P(),
    )
    return jax.shard_map(shards, mesh=mesh, in_specs=in_specs, out_specs=out_specs, check_vma=False)
```

```python
import jax
import jax.numpy as jnp
from jax import lax
from jax.experimental import pallas as pl
from jax.experimental.pallas import tpu as pltpu
from jax.sharding import PartitionSpec as P

HD = 64
LEN = 1024
QB = 256
SCALE = 0.125
NEG = -1e30
F32 = jnp.float32
BF16 = jnp.bfloat16


eps = 1e-05


def normalize(values_in, gain_vec, shift_vec):
    row_mean = jnp.mean(values_in, axis=-1, keepdims=True)
    centred = values_in - row_mean
    row_var = jnp.mean(centred * centred, axis=-1, keepdims=True)
    return centred * lax.rsqrt(row_var + eps) * gain_vec + shift_vec


def gelu_tanh(hidden):
    return jax.nn.gelu(hidden, approximate=True)


def dot(left, right):
    return jnp.dot(left, right, preferred_element_type=F32)


def contract_rows(left, right):
    return lax.dot_general(left, right, (((0,), (0,)), ((), ())), preferred_element_type=F32)


def contract_cols(left, right):
    return lax.dot_general(left, right, (((1,), (1,)), ((), ())), preferred_element_type=F32)


def probs_columns(query_block, keys, first_row):
    scores = contract_cols(keys, query_block)
    key_ids = lax.broadcasted_iota(jnp.int32, scores.shape, 0)
    row_ids = first_row + lax.broadcasted_iota(jnp.int32, scores.shape, 1)
    scores = jnp.where(key_ids <= row_ids, scores, NEG)
    exp_scores = jnp.exp(scores - jnp.max(scores, axis=0, keepdims=True))
    return exp_scores * (1.0 / jnp.sum(exp_scores, axis=0, keepdims=True))


def forward_kernel(qkv_ref, out_ref):
    for head in range(2):
        base = head * 3 * HD
        for block in range(LEN // QB):
            lo, hi = block * QB, (block + 1) * QB
            queries = qkv_ref[lo:hi, base : base + HD] * SCALE
            keys = qkv_ref[:hi, base + HD : base + 2 * HD]
            values = qkv_ref[:hi, base + 2 * HD : base + 3 * HD]
            probs = probs_columns(queries, keys, lo).astype(BF16)
            out_ref[lo:hi, head * HD : (head + 1) * HD] = contract_rows(values, probs).T.astype(BF16)


def backward_kernel(qkv_ref, grad_ref, out_ref, key_acc, value_acc):
    for head in range(2):
        base = head * 3 * HD
        for block in reversed(range(LEN // QB)):
            lo, hi = block * QB, (block + 1) * QB
            queries = qkv_ref[lo:hi, base : base + HD] * SCALE
            keys = qkv_ref[:hi, base + HD : base + 2 * HD]
            values = qkv_ref[:hi, base + 2 * HD : base + 3 * HD]
            grads = grad_ref[lo:hi, head * HD : (head + 1) * HD]
            probs = probs_columns(queries, keys, lo)
            prob_grad = contract_cols(values, grads)
            row_dot = jnp.sum(probs * prob_grad, axis=0, keepdims=True)
            score_grad = (probs * (prob_grad - row_dot)).astype(BF16)
            query_grad = (contract_rows(keys, score_grad) * SCALE).T
            out_ref[lo:hi, base : base + HD] = query_grad.astype(BF16)
            key_part = dot(score_grad, queries)
            value_part = dot(probs.astype(BF16), grads)
            if hi == LEN:
                key_acc[...] = key_part
                value_acc[...] = value_part
            else:
                key_acc[:hi, :] += key_part
                value_acc[:hi, :] += value_part
        out_ref[:, base + HD : base + 2 * HD] = key_acc[...].astype(BF16)
        out_ref[:, base + 2 * HD : base + 3 * HD] = value_acc[...].astype(BF16)


def attention_cost(qkv, products):
    rows, columns = qkv.shape
    pairs = rows * LEN * (columns // (3 * HD))
    return pl.CostEstimate(
        flops=products * pairs * HD * 4, bytes_accessed=4 * rows * columns, transcendentals=pairs
    )


def attend_forward(qkv):
    rows, columns = qkv.shape
    return pl.pallas_call(
        forward_kernel,
        grid=(rows // LEN, columns // (6 * HD)),
        in_specs=[pl.BlockSpec((LEN, 6 * HD), lambda s, h: (s, h))],
        out_specs=pl.BlockSpec((LEN, 2 * HD), lambda s, h: (s, h)),
        out_shape=jax.ShapeDtypeStruct((rows, columns // 3), BF16),
        compiler_params=pltpu.CompilerParams(vmem_limit_bytes=40 * 2**20),
        cost_estimate=attention_cost(qkv, 2),
    )(qkv)


def attend_backward(qkv, heads_grad):
    rows, columns = qkv.shape
    return pl.pallas_call(
        backward_kernel,
        grid=(rows // LEN, columns // (6 * HD)),
        in_specs=[
            pl.BlockSpec((LEN, 6 * HD), lambda s, h: (s, h)),
            pl.BlockSpec((LEN, 2 * HD), lambda s, h: (s, h)),
        ],
        out_specs=pl.BlockSpec((LEN, 6 * HD), lambda s, h: (s, h)),
        out_shape=jax.ShapeDtypeStruct((rows, columns), BF16),
        scratch_shapes=[pltpu.VMEM((LEN, HD), F32), pltpu.VMEM((LEN, HD), F32)],
        compiler_params=pltpu.CompilerParams(vmem_limit_bytes=40 * 2**20),
        cost_estimate=attention_cost(qkv, 5),
    )(qkv, heads_grad)


def swap(values):
    return lax.ppermute(values, "tensor", [(0, 1), (1, 0)])


def total_over(values, axis):
    size = lax.axis_size(axis)
    if size & (size - 1):
        return lax.psum(values, axis)
    step = 1
    while step < size:
        values = values + lax.ppermute(values, axis, [(i, i ^ step) for i in range(size)])
        step *= 2
    return values


def is_power(size):
    return size & (size - 1) == 0


def partner_swap(values, axis, size, step):
    return lax.ppermute(values, axis, [(i, i ^ step) for i in range(size)])


def gather_rows(shard, axis):
    size = lax.axis_size(axis)
    if not is_power(size):
        return lax.all_gather(shard, axis, axis=0, tiled=True)
    rows, columns = shard.shape
    me = lax.axis_index(axis)
    block = shard[None]
    step = size // 2
    while step:
        other = partner_swap(block, axis, size, step)
        upper = (me & step) != 0
        block = jnp.where(
            upper, jnp.stack((other, block), axis=1), jnp.stack((block, other), axis=1)
        ).reshape(-1, rows, columns)
        step //= 2
    return block.reshape(size * rows, columns)


def scatter_rows(full, axis):
    size = lax.axis_size(axis)
    if not is_power(size):
        return lax.psum_scatter(full, axis, scatter_dimension=0, tiled=True).astype(F32)
    rows, columns = full.shape[0] // size, full.shape[1]
    me = lax.axis_index(axis)
    block = full.reshape(size, rows, columns)
    step = 1
    while step < size:
        pairs = block.astype(BF16).reshape(-1, 2, rows, columns)
        upper = (me & step) != 0
        keep = jnp.where(upper, pairs[:, 1], pairs[:, 0])
        send = jnp.where(upper, pairs[:, 0], pairs[:, 1])
        block = keep.astype(F32) + partner_swap(send, axis, size, step).astype(F32)
        step *= 2
    return block.reshape(rows, columns).astype(F32)


class Pair:
    def __init__(self):
        self.first = lax.axis_index("tensor") == 0

    def gather(self, mine):
        return (mine, swap(mine))

    def ordered(self, parts):
        mine, other = parts
        return jnp.where(
            self.first, jnp.concatenate((mine, other)), jnp.concatenate((other, mine))
        )

    def split(self, rows):
        top, low = jnp.split(rows, 2)
        return (jnp.where(self.first, top, low), jnp.where(self.first, low, top))

    def scatter(self, parts, product, beside=()):
        mine, other = parts
        theirs = swap(product(other).astype(BF16))
        if beside:
            theirs = lax.optimization_barrier((theirs,) + beside)[0]
        return product(mine) + theirs.astype(F32)


class Group:
    def gather(self, mine):
        return (lax.all_gather(mine, "tensor", axis=0, tiled=True),)

    def ordered(self, parts):
        return parts[0]

    def split(self, rows):
        return (rows,)

    def scatter(self, parts, product, beside=()):
        summed = lax.psum_scatter(
            product(parts[0]).astype(BF16), "tensor", scatter_dimension=0, tiled=True
        )
        return summed.astype(F32)


def shards(
    inputs,
    qkv_weight,
    qv_bias,
    out_weight,
    out_bias,
    up_weight,
    up_bias,
    down_weight,
    down_bias,
    gain_one,
    shift_one,
    gain_two,
    shift_two,
    cotangent,
):
    group = Pair() if lax.axis_size("tensor") == 2 else Group()
    join = lambda parts: jnp.concatenate(parts) if len(parts) > 1 else parts[0]
    each = lambda fn, parts: tuple(fn(part) for part in parts)
    local_x = inputs.astype(F32)
    head_count = qv_bias.shape[0] // (2 * HD)
    first_norm = normalize(local_x, gain_one, shift_one).astype(BF16)
    first_parts = group.gather(first_norm)
    qkv_full = lax.all_gather(qkv_weight, "dp", axis=0, tiled=True)
    out_turned = gather_rows(out_weight.T, "dp")
    up_full = gather_rows(up_weight, "dp")
    down_full = lax.all_gather(down_weight, "dp", axis=1, tiled=True)
    biases = qv_bias.reshape(head_count, 2, HD)
    qkv_bias = jnp.stack(
        (biases[:, 0], jnp.zeros_like(biases[:, 0]), biases[:, 1]), axis=1
    ).reshape(-1)
    qkv = group.ordered(
        each(lambda rows: (dot(rows, qkv_full) + qkv_bias).astype(BF16), first_parts)
    )
    down_parts = group.gather(cotangent)
    qkv = lax.optimization_barrier((qkv,) + down_parts)[0]
    heads_low = attend_forward(qkv)
    heads_parts = group.split(heads_low)
    branch = group.scatter(heads_parts, lambda rows: contract_cols(rows, out_turned)) + out_bias
    middle = local_x + branch
    second_norm = normalize(middle, gain_two, shift_two).astype(BF16)
    second_parts = group.gather(second_norm)
    hidden = each(lambda rows: dot(rows, up_full) + up_bias, second_parts)
    active = each(lambda rows: gelu_tanh(rows).astype(BF16), hidden)

    out_grad = cotangent.astype(F32)
    down_bias_grad = jnp.sum(out_grad, axis=0)

    def hidden_back(pair_in):
        rows, grads = pair_in
        active_grad = contract_cols(grads, down_full)
        return jax.vjp(gelu_tanh, rows)[1](active_grad)[0].astype(BF16)

    hidden_parts = each(hidden_back, tuple(zip(hidden, down_parts)))
    down_weight_grad = contract_rows(join(active), join(down_parts)).astype(BF16)
    down_shard = lax.psum_scatter(down_weight_grad, "dp", scatter_dimension=1, tiled=True)
    hidden_low = join(hidden_parts)
    up_bias_grad = jnp.sum(hidden_low, axis=0, dtype=F32)
    up_weight_grad = contract_rows(join(second_parts), hidden_low).astype(BF16)
    second_grad = group.scatter(
        hidden_parts,
        lambda rows: contract_cols(rows, up_full),
        (down_weight_grad, up_weight_grad),
    )
    up_shard = scatter_rows(up_weight_grad, "dp")
    norm_pull = jax.vjp(normalize, middle, gain_two, shift_two)[1]
    middle_part, gain_two_grad, shift_two_grad = norm_pull(second_grad)
    middle_grad = out_grad + middle_part
    branch_low = middle_grad.astype(BF16)
    out_bias_grad = jnp.sum(branch_low, axis=0, dtype=F32)
    branch_parts = group.gather(branch_low)
    heads_grad = group.ordered(
        each(lambda rows: dot(rows, out_turned).astype(BF16), branch_parts)
    )
    late_active = lax.optimization_barrier(active + (heads_grad,))[:-1]
    down_out = group.scatter(late_active, lambda rows: dot(rows, down_full)) + down_bias
    layer_out = (middle + down_out).astype(BF16)
    out_weight_grad = contract_rows(join(branch_parts), join(heads_parts)).astype(BF16)
    out_shard = scatter_rows(out_weight_grad, "dp").T
    qkv_low = attend_backward(qkv, heads_grad)
    qkv_parts = group.split(qkv_low)
    qkv_weight_grad = contract_rows(join(first_parts), join(qkv_parts)).astype(BF16)
    qkv_shard = scatter_rows(qkv_weight_grad, "dp")
    first_grad = group.scatter(qkv_parts, lambda rows: contract_cols(rows, qkv_full))
    bias_sums = jnp.sum(qkv_low, axis=0, dtype=F32).reshape(head_count, 3, HD)
    qv_bias_grad = jnp.stack((bias_sums[:, 0], bias_sums[:, 2]), axis=1).reshape(-1)
    first_pull = jax.vjp(normalize, local_x, gain_one, shift_one)[1]
    input_part, gain_one_grad, shift_one_grad = first_pull(first_grad)
    input_grad = middle_grad + input_part

    width = out_bias.shape[0]
    shared = jnp.concatenate(
        (
            out_bias_grad,
            down_bias_grad,
            gain_two_grad,
            shift_two_grad,
            gain_one_grad,
            shift_one_grad,
        )
    )
    owned = jnp.concatenate((qv_bias_grad, up_bias_grad))
    shared = total_over(shared, "tensor")
    totals = total_over(jnp.concatenate((shared, owned)).reshape(-1, 128), "dp").reshape(-1)
    out_bias_total, down_bias_total, gain_two_total, shift_two_total, gain_one_total, shift_one_total = (
        jnp.split(totals[: 6 * width], 6)
    )
    qv_bias_total, up_bias_total = jnp.split(totals[6 * width :], [qv_bias.shape[0]])
    return (
        layer_out,
        input_grad,
        qkv_shard.astype(F32),
        qv_bias_total,
        out_shard.astype(F32),
        out_bias_total,
        up_shard.astype(F32),
        up_bias_total,
        down_shard.astype(F32),
        down_bias_total,
        gain_one_total,
        shift_one_total,
        gain_two_total,
        shift_two_total,
    )


def solution(mesh):
    in_specs = (
        P(("dp", "tensor"), None),
        P("dp", "tensor"),
        P("tensor"),
        P("tensor", "dp"),
        P(),
        P("dp", "tensor"),
        P("tensor"),
        P("tensor", "dp"),
        P(),
        P(),
        P(),
        P(),
        P(),
        P(("dp", "tensor"), None),
    )
    out_specs = (
        P(("dp", "tensor"), None),
        P(("dp", "tensor"), None),
        P("dp", "tensor"),
        P("tensor"),
        P("tensor", "dp"),
        P(),
        P("dp", "tensor"),
        P("tensor"),
        P("tensor", "dp"),
        P(),
        P(),
        P(),
        P(),
        P(),
    )
    return jax.shard_map(shards, mesh=mesh, in_specs=in_specs, out_specs=out_specs, check_vma=False)
```
